512 devices in a mesh: ha: 8 (over y_lo, core), wa: 16 (over y_hi, z), hd: 4 (over x).
Axes of the slice: x: 4, y: 8 (y_hi: 2, y_lo: 4; y = y_hi * 4 + y_lo), z: 8, core: 2. Of those that a mesh axis runs over, the one named last changes fastest.
Arguments:
- q_raw: bfloat16 [8, 16, 128, 2560], P('ha', 'wa', None, 'hd')
- k_raw: bfloat16 [8, 16, 128, 2560], P('ha', 'wa', None, 'hd')
- values: bfloat16 [8, 16, 128, 2560], P('ha', 'wa', None, 'hd')
- upstream: bfloat16 [8, 16, 128, 2560], P('ha', 'wa', None, 'hd'), may hold values from -384 to 384
- outputs: bfloat16 [8, 16, 128, 2560], P('ha', 'wa', None, 'hd')
- logsumexp: float32 [8, 16, 20, 128], P('ha', 'wa', 'hd'), may hold values from 7.5 to 9.5
- gain_q: bfloat16 [2560], P('hd'), may hold values from 0.25 to 1.75
- gain_k: bfloat16 [2560], P('hd'), may hold values from 0.25 to 1.75
- far_list: int32 [8, 16, 12], P('ha'), may hold values from -1 to 63, as said below
Outputs:
- dq_raw: bfloat16 [8, 16, 128, 2560], P('ha', 'wa', None, 'hd')
- dk_raw: bfloat16 [8, 16, 128, 2560], P('ha', 'wa', None, 'hd')
- dv: bfloat16 [8, 16, 128, 2560], P('ha', 'wa', None, 'hd')
The draws below stay inside these ranges and needn't reach their ends.
Inputs may be any that keep to these rules, and one draw needn't show every extreme that they name: far_list[r, c, f] is -1 (an empty slot) or names key unit u of tile (r, u // 4); the named tiles lie two or more columns away from c, and each is named at most once in far_list[r, c].
All inputs are finite; a program needn't handle non-finite values.
Results may differ from the reference program's by a relative error of at most 0.0015.
The reference program's roundings to bfloat16 on the way (of `dscore`, `weight_low`, `dq_norm` and `dk_norm`) count: a program that leaves them out, or rounds other values in their place, can miss the bound.
Values may be sent and summed in bfloat16 or wider, within the bound.
No kernel may reach another device: no remote copies, remote signals or barrier semaphores. Data moves between devices by JAX's collectives and lax.ppermute only.
A program may use at most 64 MiB of HBM per device.

```python
import math
import jax
import jax.numpy as jnp
from jax import lax

HEADS = 20
HEAD = 128
TOK_DEV = 128
UNITS = 4
FAR = 12
TROWS = 8
TCOLS = 16
HW = 2560
KB = 32


def ramp_draw(key):
    shape = (TROWS, TCOLS, TOK_DEV, HW)
    head_place = (jnp.arange(HW) // HEAD).astype(jnp.float32) / max(HEADS - 1, 1)
    parts = jax.random.split(key, 1)
    base = jax.random.normal(parts[0], shape, jnp.float32)
    ramp = jnp.exp(0.5 * math.log(3.0) * head_place)
    return (base * ramp).astype(jnp.bfloat16)


def draw_q_raw(key, part):
    return ramp_draw(jax.random.fold_in(key, 101))


def draw_k_raw(key, part):
    return ramp_draw(jax.random.fold_in(key, 202))


def channel_mean(key):
    return jax.random.normal(jax.random.fold_in(key, 303), (HW,), jnp.float32)


def noise_draw(key):
    shape = (TROWS, TCOLS, TOK_DEV, HW)
    return jax.random.normal(key, shape, jnp.float32)


def draw_values(key, part):
    return (channel_mean(key) + noise_draw(jax.random.fold_in(key, 404))).astype(jnp.bfloat16)


def draw_outputs(key, part):
    return (channel_mean(key) + 0.15 * noise_draw(jax.random.fold_in(key, 505))).astype(jnp.bfloat16)


def draw_far_list(key, part):
    parts = jax.random.split(jax.random.fold_in(key, 606), 4)
    owners = jnp.arange(TCOLS, dtype=jnp.int32)
    column = owners[None, :, None]
    peer = owners[None, None, :]
    popularity = jax.random.randint(parts[0], (TROWS, 1, TCOLS), 0, TCOLS)
    jitter = jax.random.randint(parts[1], (TROWS, TCOLS, TCOLS), 0, TCOLS)
    score = 2 * popularity + jitter
    eligible = jnp.abs(peer - column) >= 2
    score = jnp.where(eligible, score, 4 * TCOLS)
    forced = (column == 0) & (peer == TCOLS - 1)
    score = jnp.where(forced, -1, score)
    ranked = jnp.argsort(score * TCOLS + peer, axis=-1, stable=True).astype(jnp.int32)
    filler = jnp.zeros((TROWS, TCOLS, FAR), jnp.int32)
    ranked = jnp.concatenate([ranked, filler], axis=-1)[..., :FAR]
    available = jnp.broadcast_to(jnp.sum(eligible, axis=-1).astype(jnp.int32), (TROWS, TCOLS))
    wanted = jax.random.randint(parts[2], (TROWS, TCOLS), max(FAR - 2, 1), FAR + 1)
    wanted = jnp.where(owners[None, :] == 1, max(FAR - 2, 1), wanted)
    count = jnp.minimum(wanted, available)
    slot = jnp.arange(FAR, dtype=jnp.int32)
    unit = jax.random.randint(parts[3], (TROWS, TCOLS, FAR), 0, UNITS)
    unit = jnp.where((owners[None, :, None] == 0) & (slot[None, None, :] == 0), UNITS - 1, unit)
    return jnp.where(slot[None, None, :] < count[..., None], ranked * UNITS + unit, -1).astype(jnp.int32)


def shard_levels(own_key, extent, pieces, smallest, high):
    def one(position, blocks):
        draws = jax.random.uniform(jax.random.fold_in(jax.random.fold_in(own_key, 6), position), (blocks,), jnp.float32, smallest / len(pieces), high / len(pieces))
        return jnp.repeat(jnp.exp(draws), extent[position] // blocks).reshape((-1,) + (1,) * (len(extent) - position - 1))

    loudness = one(*pieces[0])
    for cut in pieces[1:]:
        loudness = loudness * one(*cut)
    return loudness


def bell_draw(key, extent, deviation, most, pieces=(), kind=jnp.bfloat16):
    result = jax.random.normal(key, extent, jnp.float32) * deviation
    if len(pieces) > 0:
        result = shard_levels(key, extent, pieces, -0.22, 0.18) * result
    return jnp.clip(result, min=-most, max=most).astype(kind)


def setup_inputs(seed: int = 0) -> dict:
    streams_of = jax.random.split(jax.random.key(seed), 10)
    return {
        "q_raw": draw_q_raw(jax.random.fold_in(streams_of[9], 71), 0),
        "k_raw": draw_k_raw(jax.random.fold_in(streams_of[9], 71), 0),
        "values": draw_values(jax.random.fold_in(streams_of[9], 71), 0),
        "upstream": bell_draw(streams_of[3], (TROWS, TCOLS, TOK_DEV, HW), 64.0, 384.0, ((0, 8), (1, 16), (3, 4))),
        "outputs": draw_outputs(jax.random.fold_in(streams_of[9], 71), 0),
        "logsumexp": jnp.clip(7.5 + 2.0 * jax.random.uniform(streams_of[5], (TROWS, TCOLS, HEADS, TOK_DEV), jnp.float32) ** shard_levels(streams_of[5], (TROWS, TCOLS, HEADS, TOK_DEV), ((0, 8), (1, 16), (2, 4)), -0.2, 0.2), 7.5, 9.5),
        "gain_q": jnp.clip(1.0 + 0.15 * jax.random.normal(streams_of[6], (HW,), jnp.float32), 0.25, 1.75).astype(jnp.bfloat16),
        "gain_k": jnp.clip(1.0 + 0.15 * jax.random.normal(streams_of[7], (HW,), jnp.float32), 0.25, 1.75).astype(jnp.bfloat16),
        "far_list": draw_far_list(jax.random.fold_in(streams_of[9], 71), 0),
    }


EPS = 1e-06
POSITIONS = ((1, 1), (0, 1), (2, 1), (1, 0), (1, 2))

def rounded(array):
    return lax.optimization_barrier(array.astype(jnp.bfloat16)).astype(jnp.float32)

def norm_rows(raw, gain):
    raw_wide = raw.astype(jnp.float32)
    rate = lax.rsqrt(lax.optimization_barrier(jnp.mean(raw_wide * raw_wide, axis=-1)) + EPS)
    return ((raw_wide * rate[..., None] * gain.astype(jnp.float32)).astype(jnp.bfloat16), rate)

def block_terms(queries, upstream_tile, lse_tile, delta_tile, keys, vals, key_valid):
    query_count = queries.shape[0]
    key_count = keys.shape[0]
    query_heads = queries.astype(jnp.float32).reshape(query_count, HEADS, HEAD)
    upstream_heads = upstream_tile.astype(jnp.float32).reshape(query_count, HEADS, HEAD)
    key_heads = keys.astype(jnp.float32).reshape(key_count, HEADS, HEAD)
    value_heads = vals.astype(jnp.float32).reshape(key_count, HEADS, HEAD)
    scores = jnp.einsum('ihd,jhd->hij', query_heads, key_heads) / math.sqrt(HEAD)
    weight = jnp.where(key_valid[None, None, :], jnp.exp(scores - lse_tile[:, :, None]), 0.0)
    dweight = jnp.einsum('ihd,jhd->hij', upstream_heads, value_heads)
    dscore = rounded(weight * (dweight - delta_tile[:, :, None]))
    weight_low = rounded(weight)
    return (query_heads, upstream_heads, key_heads, dscore, weight_low)

def query_side(queries, upstream_tile, lse_tile, delta_tile, keys, vals, key_valid):
    query_heads, upstream_heads, key_heads, dscore, weight_low = block_terms(queries, upstream_tile, lse_tile, delta_tile, keys, vals, key_valid)
    grads = jnp.einsum('hij,jhd->ihd', dscore, key_heads) / math.sqrt(HEAD)
    return grads.reshape(queries.shape[0], HW).astype(jnp.bfloat16)

def key_side(queries, upstream_tile, lse_tile, delta_tile, keys, vals, key_valid):
    query_heads, upstream_heads, key_heads, dscore, weight_low = block_terms(queries, upstream_tile, lse_tile, delta_tile, keys, vals, key_valid)
    key_grads = jnp.einsum('hij,ihd->jhd', dscore, query_heads) / math.sqrt(HEAD)
    value_grads = jnp.einsum('hij,ihd->jhd', weight_low, upstream_heads)
    count = keys.shape[0]
    return (key_grads.reshape(count, HW).astype(jnp.bfloat16), value_grads.reshape(count, HW).astype(jnp.bfloat16))

def pick(array, row, col):
    inner = lax.dynamic_index_in_dim(array, row, 0, keepdims=False)
    return lax.dynamic_index_in_dim(inner, col, 0, keepdims=False)

def tile_exists(row, col):
    return (row >= 0) & (row < TROWS) & (col >= 0) & (col < TCOLS)

def reference(q_raw, k_raw, values, upstream, outputs, logsumexp, gain_q, gain_k, far_list):
    query_norm, q_rate = norm_rows(q_raw, gain_q)
    key_norm, k_rate = norm_rows(k_raw, gain_k)
    product = upstream.astype(jnp.float32) * outputs.astype(jnp.float32)
    delta = lax.optimization_barrier(jnp.sum(product.reshape(TROWS, TCOLS, TOK_DEV, HEADS, HEAD), axis=-1)).transpose(0, 1, 3, 2)
    padding = ((1, 1), (1, 1), (0, 0), (0, 0))
    key_pad = jnp.pad(key_norm, padding)
    value_pad = jnp.pad(values, padding)
    query_pad = jnp.pad(query_norm, padding)
    upstream_pad = jnp.pad(upstream, padding)
    lse_pad = jnp.pad(logsumexp, padding)
    delta_pad = jnp.pad(delta, padding)

    def query_tile(flat):
        row = (flat // TCOLS).astype(jnp.int32)
        col = (flat % TCOLS).astype(jnp.int32)
        win_keys = jnp.concatenate([pick(key_pad, row + row_step, col + col_step) for row_step, col_step in POSITIONS], 0)
        win_vals = jnp.concatenate([pick(value_pad, row + row_step, col + col_step) for row_step, col_step in POSITIONS], 0)
        win_valid = jnp.concatenate([jnp.broadcast_to(tile_exists(row + row_step - 1, col + col_step - 1), (TOK_DEV,)) for row_step, col_step in POSITIONS], 0)
        listed = pick(far_list, row, col)
        safe = jnp.maximum(listed, 0)
        owner = (safe // UNITS).astype(jnp.int32)
        first = (safe % UNITS * KB).astype(jnp.int32)

        def one_unit(owner_col, start):
            unit_keys = lax.dynamic_slice_in_dim(pick(key_norm, row, owner_col), start, KB, 0)
            unit_vals = lax.dynamic_slice_in_dim(pick(values, row, owner_col), start, KB, 0)
            return (unit_keys, unit_vals)
        far_keys, far_vals = jax.vmap(one_unit)(owner, first)
        keys = jnp.concatenate([win_keys, far_keys.reshape(FAR * KB, HW)], 0)
        vals = jnp.concatenate([win_vals, far_vals.reshape(FAR * KB, HW)], 0)
        valid = jnp.concatenate([win_valid, jnp.repeat(listed >= 0, KB)], 0)
        return query_side(pick(query_norm, row, col), pick(upstream, row, col), pick(logsumexp, row, col), pick(delta, row, col), keys, vals, valid)
    tiles = jnp.arange(TROWS * TCOLS, dtype=jnp.int32)
    dq_norm = lax.map(query_tile, tiles).reshape(TROWS, TCOLS, TOK_DEV, HW)

    def key_tile(flat):
        row = (flat // TCOLS).astype(jnp.int32)
        col = (flat % TCOLS).astype(jnp.int32)
        own_keys = pick(key_norm, row, col)
        own_vals = pick(values, row, col)
        total_key = jnp.zeros((TOK_DEV, HW), jnp.float32)
        total_value = jnp.zeros((TOK_DEV, HW), jnp.float32)
        for row_step, col_step in POSITIONS:
            valid = jnp.broadcast_to(tile_exists(row + row_step - 1, col + col_step - 1), (TOK_DEV,))
            part_key, part_value = key_side(pick(query_pad, row + row_step, col + col_step), pick(upstream_pad, row + row_step, col + col_step), pick(lse_pad, row + row_step, col + col_step), pick(delta_pad, row + row_step, col + col_step), own_keys, own_vals, valid)
            total_key = total_key + part_key.astype(jnp.float32)
            total_value = total_value + part_value.astype(jnp.float32)

        def add_far(source, carry):
            sum_key, sum_value = carry
            source = jnp.asarray(source).astype(jnp.int32)
            listed = pick(far_list, row, source)
            asked = (listed >= 0) & (listed // UNITS == col)
            present = jnp.any(asked)
            unit = jnp.sum(jnp.where(asked, listed % UNITS, 0)).astype(jnp.int32)
            unit_keys = lax.dynamic_slice_in_dim(own_keys, unit * KB, KB, 0)
            unit_vals = lax.dynamic_slice_in_dim(own_vals, unit * KB, KB, 0)
            part_key, part_value = key_side(pick(query_norm, row, source), pick(upstream, row, source), pick(logsumexp, row, source), pick(delta, row, source), unit_keys, unit_vals, jnp.broadcast_to(present, (KB,)))
            place = (jnp.arange(UNITS, dtype=jnp.int32) == unit).astype(jnp.float32)
            sum_key = sum_key + place[:, None, None] * part_key.astype(jnp.float32)[None]
            sum_value = sum_value + place[:, None, None] * part_value.astype(jnp.float32)[None]
            return (sum_key, sum_value)
        empty = jnp.zeros((UNITS, KB, HW), jnp.float32)
        far_key, far_value = lax.fori_loop(0, TCOLS, add_far, (empty, empty))
        key_grad = (total_key + far_key.reshape(TOK_DEV, HW)).astype(jnp.bfloat16)
        value_grad = (total_value + far_value.reshape(TOK_DEV, HW)).astype(jnp.bfloat16)
        return (key_grad, value_grad)
    dk_norm, dv = lax.map(key_tile, tiles)
    dk_norm = dk_norm.reshape(TROWS, TCOLS, TOK_DEV, HW)
    dv = dv.reshape(TROWS, TCOLS, TOK_DEV, HW)
    gain_qw = gain_q.astype(jnp.float32)
    gain_kw = gain_k.astype(jnp.float32)
    q_wide = q_raw.astype(jnp.float32)
    k_wide = k_raw.astype(jnp.float32)
    dq_wide = dq_norm.astype(jnp.float32)
    dk_wide = dk_norm.astype(jnp.float32)
    q_dot = lax.optimization_barrier(jnp.sum(gain_qw * dq_wide * q_wide, axis=-1))
    k_dot = lax.optimization_barrier(jnp.sum(gain_kw * dk_wide * k_wide, axis=-1))
    dq_raw = (q_rate[..., None] * gain_qw * dq_wide - q_wide * (q_rate ** 3 * q_dot / HW)[..., None]).astype(jnp.bfloat16)
    dk_raw = (k_rate[..., None] * gain_kw * dk_wide - k_wide * (k_rate ** 3 * k_dot / HW)[..., None]).astype(jnp.bfloat16)
    return (dq_raw, dk_raw, dv)
```

```python
import functools
import math

import jax
import jax.numpy as jnp
from jax import lax
from jax.experimental import pallas as pl
from jax.experimental.pallas import tpu as pltpu
from jax.sharding import PartitionSpec as P

HEAD = 128
UNITS = 4
KEYS = 32
HALF = 8
EPS = 1e-06
LIMIT = 40 * 1024 * 1024
SCALE = 1.0 / math.sqrt(HEAD)
BOTH_LAST = (((1,), (1,)), ((), ()))
BOTH_FIRST = (((0,), (0,)), ((), ()))
F32 = jnp.float32
BF16 = jnp.bfloat16

VMEM = pl.BlockSpec(memory_space=pltpu.VMEM)
SMEM = pl.BlockSpec(memory_space=pltpu.SMEM)


def local_call(kernel, out_shape, in_specs, scratch=(), flops=0, moved=0):
    return pl.pallas_call(
        kernel,
        out_shape=out_shape,
        in_specs=in_specs,
        out_specs=jax.tree.map(lambda _: VMEM, out_shape),
        scratch_shapes=list(scratch),
        compiler_params=pltpu.CompilerParams(vmem_limit_bytes=LIMIT),
        cost_estimate=pl.CostEstimate(flops=flops, bytes_accessed=moved, transcendentals=0),
    )


def cols(head):
    return slice(head * HEAD, (head + 1) * HEAD)


def tall(row):
    return jnp.broadcast_to(row, (HEAD, HEAD)).T


def square_kernel(q_ref, k_ref, out_ref):
    heads = q_ref.shape[1] // HEAD
    for place, ref in enumerate((q_ref, k_ref)):
        total = jnp.zeros((HEAD, HEAD), F32)
        for head in range(heads):
            wide = ref[:, cols(head)].astype(F32)
            total = total + wide * wide
        out_ref[place : place + 1, :] = jnp.sum(total.T, axis=0, keepdims=True)


def pack_kernel(
    unit_ref, q_ref, k_ref, v_ref, up_ref, out_ref, lse_ref, rate_ref, gain_q_ref, gain_k_ref,
    qu_ref, kv_ref, packed_ref, delta_ref,
):
    heads = q_ref.shape[1] // HEAD
    tokens = q_ref.shape[0]
    q_rate = tall(rate_ref[0:1, :])
    k_rate = tall(rate_ref[1:2, :])
    row = lax.broadcasted_iota(jnp.int32, (16, HEAD), 0)
    for head in range(heads):
        part = cols(head)
        kv_ref[0, :, part] = (
            k_ref[:, part].astype(F32) * k_rate * gain_k_ref[0:1, part].astype(F32)
        ).astype(BF16)
        qu_ref[0:tokens, part] = (
            q_ref[:, part].astype(F32) * q_rate * gain_q_ref[0:1, part].astype(F32)
        ).astype(BF16)
    kv_ref[1] = v_ref[...]
    qu_ref[tokens : 2 * tokens, :] = up_ref[...]
    for head in range(heads):
        part = cols(head)
        product = up_ref[:, part].astype(F32) * out_ref[:, part].astype(F32)
        delta = jnp.sum(product.T, axis=0, keepdims=True)
        delta_ref[0:1, part] = delta
        extra = jnp.zeros((16, HEAD), F32)
        for place, value in ((0, lse_ref[0:1, part]), (3, delta)):
            first = value.astype(BF16).astype(F32)
            rest = value - first
            second = rest.astype(BF16).astype(F32)
            third = rest - second
            for step, piece in enumerate((first, second, third)):
                extra = jnp.where(row == place + step, piece, extra)
        qu_ref[2 * tokens : 2 * tokens + 16, part] = extra.astype(BF16)
    for peer in range(HALF):
        for side in range(2):
            start = pl.multiple_of(unit_ref[side, peer] * KEYS, KEYS)
            base = side * 2 * KEYS
            packed_ref[peer, base : base + KEYS, :] = kv_ref[0, pl.ds(start, KEYS), :]
            packed_ref[peer, base + KEYS : base + 2 * KEYS, :] = kv_ref[1, pl.ds(start, KEYS), :]


def block_grads(keys, vals, query, upstream, lse, delta):
    scores = lax.dot_general(keys, query, BOTH_LAST, preferred_element_type=F32) * SCALE
    weight = jnp.exp(scores - lse)
    dweight = lax.dot_general(vals, upstream, BOTH_LAST, preferred_element_type=F32)
    dscore = (weight * (dweight - delta)).astype(BF16)
    dkey = jnp.dot(dscore, query, preferred_element_type=F32) * SCALE
    dval = jnp.dot(weight.astype(BF16), upstream, preferred_element_type=F32)
    dquery = lax.dot_general(dscore, keys, BOTH_FIRST, preferred_element_type=F32) * SCALE
    return dkey.astype(BF16), dval.astype(BF16), dquery


def window_kernel(exists_ref, qu_ref, lse_ref, delta_ref, *refs):
    tiles, dq_ref, parts = refs[:5], refs[5], refs[6:]
    heads = lse_ref.shape[1] // HEAD
    tokens = tiles[0].shape[1]
    for head in range(heads):
        part = cols(head)
        query = qu_ref[0:tokens, part]
        upstream = qu_ref[tokens : 2 * tokens, part]
        lse = lse_ref[0:1, part]
        delta = delta_ref[0:1, part]
        total = None
        for place, (tile, out) in enumerate(zip(tiles, parts)):
            bound = lse
            if place > 0:
                bound = jnp.where(exists_ref[place] > 0, lse, jnp.inf)
            dkey, dval, dquery = block_grads(
                tile[0, :, part], tile[1, :, part], query, upstream, bound, delta
            )
            out[0, :, part] = dkey
            out[1, :, part] = dval
            total = dquery if total is None else total + dquery
        dq_ref[:, part] = total


def far_kernel(used_ref, got_ref, qu_ref, other_ref, lse_ref, delta_ref, back_ref, dq_ref, dq_other_ref):
    heads = lse_ref.shape[1] // HEAD
    tokens = dq_ref.shape[0]
    for side, (source, grad) in enumerate(((qu_ref, dq_ref), (other_ref, dq_other_ref))):
        base = side * 2 * KEYS
        for head in range(heads):
            part = cols(head)
            query = source[0:tokens, part]
            upstream = source[tokens : 2 * tokens, part]
            if side == 0:
                lse = lse_ref[0:1, part]
                delta = delta_ref[0:1, part]
            else:
                extra = source[2 * tokens : 2 * tokens + 16, part].astype(F32)
                lse = extra[0:1] + (extra[1:2] + extra[2:3])
                delta = extra[3:4] + (extra[4:5] + extra[5:6])
            bound = jnp.concatenate(
                [
                    jnp.broadcast_to(
                        jnp.where(used_ref[side, peer] > 0, lse, jnp.inf), (KEYS, HEAD)
                    )
                    for peer in range(HALF)
                ],
                axis=0,
            )
            keys = got_ref[:, base : base + KEYS, part].reshape(HALF * KEYS, HEAD)
            vals = got_ref[:, base + KEYS : base + 2 * KEYS, part].reshape(HALF * KEYS, HEAD)
            dkey, dval, dquery = block_grads(keys, vals, query, upstream, bound, delta)
            back_ref[:, base : base + KEYS, part] = dkey.reshape(HALF, KEYS, HEAD)
            back_ref[:, base + KEYS : base + 2 * KEYS, part] = dval.reshape(HALF, KEYS, HEAD)
            grad[:, part] = dquery


def sum_kernel(
    unit_ref, sent_ref, own_ref, up_ref, down_ref, left_ref, right_ref, back_ref,
    dq_win_ref, dq_far_ref, dq_got_ref, q_ref, k_ref, gain_q_ref, gain_k_ref,
    dq_ref, dk_ref, dv_ref, dots_ref, total,
):
    heads = q_ref.shape[1] // HEAD
    total[...] = (
        own_ref[...].astype(F32)
        + up_ref[...].astype(F32)
        + down_ref[...].astype(F32)
        + left_ref[...].astype(F32)
        + right_ref[...].astype(F32)
    )
    for peer in range(HALF):
        for side in range(2):
            base = side * 2 * KEYS

            @pl.when(sent_ref[side, peer] > 0)
            def _():
                start = pl.multiple_of(unit_ref[side, peer] * KEYS, KEYS)
                for kind in range(2):
                    low = base + kind * KEYS
                    total[kind, pl.ds(start, KEYS), :] += back_ref[
                        peer, low : low + KEYS, :
                    ].astype(F32)

    q_dot = jnp.zeros((HEAD, HEAD), F32)
    k_dot = jnp.zeros((HEAD, HEAD), F32)
    for head in range(heads):
        part = cols(head)
        dq = (dq_win_ref[:, part] + dq_far_ref[:, part] + dq_got_ref[:, part]).astype(BF16)
        dk = total[0, :, part].astype(BF16)
        dv_ref[:, part] = total[1, :, part].astype(BF16)
        dq_ref[:, part] = dq
        dk_ref[:, part] = dk
        q_dot = q_dot + gain_q_ref[0:1, part].astype(F32) * dq.astype(F32) * q_ref[:, part].astype(F32)
        k_dot = k_dot + gain_k_ref[0:1, part].astype(F32) * dk.astype(F32) * k_ref[:, part].astype(F32)
    dots_ref[0:1, :] = jnp.sum(q_dot.T, axis=0, keepdims=True)
    dots_ref[1:2, :] = jnp.sum(k_dot.T, axis=0, keepdims=True)


def last_kernel(
    full_width, dq_ref, dk_ref, q_ref, k_ref, gain_q_ref, gain_k_ref, rate_ref, dots_ref,
    dq_out, dk_out,
):
    heads = q_ref.shape[1] // HEAD
    for place, (grad, raw, gain, out) in enumerate(
        ((dq_ref, q_ref, gain_q_ref, dq_out), (dk_ref, k_ref, gain_k_ref, dk_out))
    ):
        rate_row = rate_ref[place : place + 1, :]
        dots = dots_ref[place : place + 1, :]
        rate = tall(rate_row)
        pull = tall(rate_row * rate_row * rate_row * dots / full_width)
        for head in range(heads):
            part = cols(head)
            out[:, part] = (
                rate * gain[0:1, part].astype(F32) * grad[:, part].astype(F32)
                - raw[:, part].astype(F32) * pull
            ).astype(BF16)


def body(q_raw, k_raw, values, upstream, outputs, logsumexp, gain_q, gain_k, far_list):
    row_index = lax.axis_index("ha")
    col_index = lax.axis_index("wa")
    rows = lax.axis_size("ha")
    columns = lax.axis_size("wa")
    q_tile, k_tile, v_tile = q_raw[0, 0], k_raw[0, 0], values[0, 0]
    up_tile, out_tile = upstream[0, 0], outputs[0, 0]
    tokens, width = q_tile.shape
    full_width = width * lax.axis_size("hd")
    lse_row = logsumexp[0, 0].reshape(1, width)
    gain_q_row = gain_q.reshape(1, width)
    gain_k_row = gain_k.reshape(1, width)

    half = col_index // HALF
    place = col_index % HALF
    lists = far_list[0]
    owner = jnp.where(lists >= 0, lists // UNITS, -1)
    asked = owner == col_index
    unit = jnp.sum(jnp.where(asked, lists % UNITS, 0), axis=1).reshape(2, HALF)
    sent = jnp.any(asked, axis=1).astype(jnp.int32).reshape(2, HALF)
    unit = jnp.where(half == 0, unit, unit[::-1])
    sent = jnp.where(half == 0, sent, sent[::-1])
    peers = half * HALF + jnp.arange(HALF, dtype=jnp.int32)
    readers = jnp.stack([half * HALF + place, (1 - half) * HALF + place])
    reader_owner = jnp.take(owner, readers, axis=0)
    used = jnp.any(reader_owner[:, None, :] == peers[None, :, None], axis=2).astype(jnp.int32)
    exists = jnp.stack(
        [
            jnp.ones((), bool),
            row_index > 0,
            row_index < rows - 1,
            col_index > 0,
            col_index < columns - 1,
        ]
    ).astype(jnp.int32)

    shape = jax.ShapeDtypeStruct
    tile_pair = shape((2, tokens, width), BF16)
    slots = shape((HALF, 4 * KEYS, width), BF16)
    wide = shape((tokens, width), F32)
    narrow = shape((tokens, width), BF16)

    squares = local_call(square_kernel, shape((2, tokens), F32), [VMEM] * 2)(q_tile, k_tile)
    squares = lax.psum(squares, "hd")
    rates = lax.rsqrt(squares / full_width + EPS)
    qu, kv, packed, delta_row = local_call(
        pack_kernel,
        (shape((2 * tokens + 16, width), BF16), tile_pair, slots, shape((1, width), F32)),
        [SMEM] + [VMEM] * 9,
    )(unit, q_tile, k_tile, v_tile, up_tile, out_tile, lse_row, rates, gain_q_row, gain_k_row)

    groups = [[h * HALF + z for z in range(HALF)] for h in range(2)]
    swap = [(c, (c + HALF) % columns) for c in range(columns)]

    def exchange(array):
        return lax.all_to_all(array, "wa", 0, 0, axis_index_groups=groups, tiled=True)

    def shifted(array, axis, step):
        count = lax.axis_size(axis)
        first, last = max(0, -step), min(count, count - step)
        return lax.ppermute(array, axis, [(i, i + step) for i in range(first, last)])

    got = exchange(packed)
    other = lax.ppermute(qu, "wa", swap)
    above = shifted(kv, "ha", 1)
    below = shifted(kv, "ha", -1)
    left = shifted(kv, "wa", 1)
    right = shifted(kv, "wa", -1)

    dq_win, own_part, up_part, down_part, left_part, right_part = local_call(
        window_kernel, (wide,) + (tile_pair,) * 5, [SMEM] + [VMEM] * 8,
        flops=10 * tokens * 5 * tokens * width, moved=4 * 1024 * 1024,
    )(exists, qu, lse_row, delta_row, kv, above, below, left, right)
    back_slots, dq_far, dq_other = local_call(
        far_kernel, (slots, wide, wide), [SMEM] + [VMEM] * 5,
        flops=10 * tokens * 4 * tokens * width, moved=4 * 1024 * 1024,
    )(used, got, qu, other, lse_row, delta_row)

    back = exchange(back_slots)
    dq_got = lax.ppermute(dq_other, "wa", swap)
    from_below = shifted(up_part, "ha", -1)
    from_above = shifted(down_part, "ha", 1)
    from_right = shifted(left_part, "wa", -1)
    from_left = shifted(right_part, "wa", 1)

    dq_norm, dk_norm, dv_tile, dots = local_call(
        sum_kernel,
        (narrow, narrow, narrow, shape((2, tokens), F32)),
        [SMEM] * 2 + [VMEM] * 13,
        scratch=[pltpu.VMEM((2, tokens, width), F32)],
    )(
        unit, sent, own_part, from_below, from_above, from_right, from_left, back,
        dq_win, dq_far, dq_got, q_tile, k_tile, gain_q_row, gain_k_row,
    )
    dots = lax.psum(dots, "hd")
    dq_tile, dk_tile = local_call(
        functools.partial(last_kernel, full_width), (narrow, narrow), [VMEM] * 8
    )(dq_norm, dk_norm, q_tile, k_tile, gain_q_row, gain_k_row, rates, dots)
    return (dq_tile[None, None], dk_tile[None, None], dv_tile[None, None])


def solution(mesh):
    tile = P("ha", "wa", None, "hd")
    return jax.shard_map(
        body,
        mesh=mesh,
        in_specs=(
            tile, tile, tile, tile, tile,
            P("ha", "wa", "hd", None), P("hd"), P("hd"), P("ha", None, None),
        ),
        out_specs=(tile, tile, tile),
        check_vma=False,
    )
```

```python
import functools
import math

import jax
import jax.numpy as jnp
from jax import lax
from jax.experimental import pallas as pl
from jax.experimental.pallas import tpu as pltpu
from jax.sharding import PartitionSpec as P

HEAD = 128
UNITS = 4
KEYS = 32
HALF = 8
EPS = 1e-06
LIMIT = 62 * 1024 * 1024
ROOMY = 59 * 1024 * 1024
SCALE = 1.0 / math.sqrt(HEAD)
BOTH_LAST = (((1,), (1,)), ((), ()))
BOTH_FIRST = (((0,), (0,)), ((), ()))
F32 = jnp.float32
BF16 = jnp.bfloat16

HBM = pl.BlockSpec(memory_space=pltpu.HBM)
SMEM = pl.BlockSpec(memory_space=pltpu.SMEM)
shape = jax.ShapeDtypeStruct


class Staged:
    def __init__(self, inputs, outputs, made, held, kept, extra, in_sems, out_sems):
        self.outputs, self.kept, self.extra = outputs, kept, extra
        self.made, self.out_sems, self.stores, self.held = made, out_sems, [], held
        self.loads = [
            [pltpu.make_async_copy(source, target, in_sems.at[n])]
            for n, (source, target) in enumerate(zip(inputs, held))
        ]
        for load in self.loads:
            load[0].start()

    def get(self, n):
        if self.loads[n]:
            self.loads[n].pop().wait()
        return self.held[n]

    def put(self, n, index=None):
        index = (slice(None),) * len(self.outputs[n].shape) if index is None else index
        copy = pltpu.make_async_copy(
            self.kept[n].at[index], self.outputs[n].at[index], self.out_sems.at[len(self.stores)]
        )
        copy.start()
        self.stores.append(copy)

    def put_heads(self, n, first, last):
        lead = (slice(None),) * (len(self.outputs[n].shape) - 1)
        self.put(n, lead + (slice(first * HEAD, last * HEAD),))

    def finish(self):
        for n in range(len(self.loads)):
            self.get(n)
        for copy in self.stores:
            copy.wait()


def staged_call(kernel, out_shape, inputs, stores, extra=(), flops=0, made=(), limit=LIMIT):
    sizes = tuple(len(g) for g in (inputs, out_shape, made, inputs, out_shape, extra))

    def run(*refs):
        groups, low = [], 0
        for size in sizes:
            groups.append(refs[low : low + size])
            low += size
        stage = Staged(*groups, *refs[low:])
        kernel(stage)
        stage.finish()

    def held(array):
        table = array.dtype == jnp.int32
        return (pltpu.SMEM if table else pltpu.VMEM)(array.shape, array.dtype)

    moved = sum(math.prod(a.shape) * a.dtype.itemsize for a in tuple(inputs) + tuple(out_shape))
    return pl.pallas_call(
        run,
        out_shape=tuple(out_shape) + tuple(made),
        in_specs=[HBM] * len(inputs),
        out_specs=(HBM,) * len(out_shape) + (SMEM,) * len(made),
        scratch_shapes=[held(a) for a in tuple(inputs) + tuple(out_shape) + tuple(extra)]
        + [pltpu.SemaphoreType.DMA((len(inputs),)), pltpu.SemaphoreType.DMA((stores,))],
        compiler_params=pltpu.CompilerParams(vmem_limit_bytes=limit),
        cost_estimate=pl.CostEstimate(flops=flops, bytes_accessed=moved, transcendentals=0),
    )(*inputs)


def cols(head):
    return slice(head * HEAD, (head + 1) * HEAD)


def tall(row):
    return jnp.broadcast_to(row, (HEAD, HEAD)).T


def row_sums(square):
    return jnp.sum(square.T, axis=0, keepdims=True)


def place_in_row():
    column = lax.axis_index("wa")
    return column, column >> 3, column & (HALF - 1)


def front_kernel(stage):
    lists, table = stage.get(4), stage.made[0]
    column, half, place = place_in_row()
    for side in range(2):
        other = half ^ side
        for peer in range(HALF):
            beside = jnp.abs(other * HALF + peer - column) == 1
            unit, sent = jnp.int32(0), beside.astype(jnp.int32)
            for slot in range(lists.shape[0]):
                entry = lists[slot, 0, other * HALF + peer]
                hit = (entry >> 2) == column
                unit = jnp.where(hit, entry & (UNITS - 1), unit)
                sent = jnp.where(hit, 1, sent)
            table[side, peer] = unit
            table[2 + side, peer] = sent
            beside = jnp.abs(other * HALF + place - half * HALF - peer) == 1
            table[4 + side, peer] = beside.astype(jnp.int32)
        for slot in range(lists.shape[0]):
            entry = lists[slot, 0, other * HALF + place]
            peer = (entry >> 2) & (HALF - 1)
            table[4 + side, peer] = jnp.where((entry >> 5) == half, 1, table[4 + side, peer])
    gains = stage.kept[1]
    for place in range(2):
        gain = stage.get(2 + place)
        for head in range(gains.shape[1] // HEAD):
            gains[place : place + 1, cols(head)] = gain[cols(head)].astype(F32).reshape(1, HEAD)
    stage.put(1)
    for place in range(2):
        total = jnp.zeros((HEAD, HEAD), F32)
        for head in range(gains.shape[1] // HEAD):
            wide = stage.get(place)[:, cols(head)].astype(F32)
            total = total + wide * wide
        stage.kept[0][place : place + 1, :] = row_sums(total)
    stage.put(0)


def norm_rate(squares, full_width):
    return lax.rsqrt(squares / full_width + EPS)


def pack_kernel(full_width, stage):
    squares, gains, raw, vals, table = (stage.get(n) for n in range(5))
    kv, rest, packed = stage.kept
    rate = tall(norm_rate(squares[1:2, :], full_width))
    for head in range(kv.shape[2] // HEAD):
        part = cols(head)
        kv[0, :, part] = (raw[:, part].astype(F32) * rate * gains[1:2, part]).astype(BF16)
    kv[1] = vals[...]
    for peer in range(HALF):
        for side in range(2):
            start = pl.multiple_of(table[side, peer] * KEYS, KEYS)
            for kind in range(2):
                low = (2 * side + kind) * KEYS
                packed[peer, low : low + KEYS, :] = kv[kind, pl.ds(start, KEYS), :]
        if peer % 4 == 3:
            stage.put(2, (slice(peer - 3, peer + 1),))
    rest[...] = kv[:, KEYS:, :]
    stage.put(0)
    stage.put(1)


def query_kernel(full_width, stage):
    squares, gains, lse, raw, up, out = (stage.get(n) for n in range(6))
    qu = stage.kept[0]
    tokens, width = raw.shape
    rate = tall(norm_rate(squares[0:1, :], full_width))
    row = lax.broadcasted_iota(jnp.int32, (16, HEAD), 0)
    for head in range(width // HEAD):
        part = cols(head)
        qu[0:tokens, part] = (raw[:, part].astype(F32) * rate * gains[0:1, part]).astype(BF16)
        qu[tokens : 2 * tokens, part] = up[:, part]
        delta = row_sums(up[:, part].astype(F32) * out[:, part].astype(F32))
        pieces = jnp.zeros((16, HEAD), F32)
        for place, value in ((0, lse[0:1, part]), (3, delta)):
            first = value.astype(BF16).astype(F32)
            rest = value - first
            second = rest.astype(BF16).astype(F32)
            for step, piece in enumerate((first, second, rest - second)):
                pieces = jnp.where(row == place + step, piece, pieces)
        qu[2 * tokens : 2 * tokens + 16, part] = pieces.astype(BF16)
    stage.put(0)


def block_grads(keys, vals, query, upstream, lse, delta):
    scores = lax.dot_general(keys, query, BOTH_LAST, preferred_element_type=F32) * SCALE
    weight = jnp.exp(scores - lse)
    dweight = lax.dot_general(vals, upstream, BOTH_LAST, preferred_element_type=F32)
    dscore = (weight * (dweight - delta)).astype(BF16)
    dkey = jnp.dot(dscore, query, preferred_element_type=F32) * SCALE
    dval = jnp.dot(weight.astype(BF16), upstream, preferred_element_type=F32)
    dquery = lax.dot_general(dscore, keys, BOTH_FIRST, preferred_element_type=F32) * SCALE
    return dkey.astype(BF16), dval.astype(BF16), dquery


def read_query(ref, part):
    tokens = (ref.shape[0] - 16) // 2
    pieces = ref[2 * tokens : 2 * tokens + 16, part].astype(F32)
    lse = pieces[0:1] + (pieces[1:2] + pieces[2:3])
    delta = pieces[3:4] + (pieces[4:5] + pieces[5:6])
    return ref[0:tokens, part], ref[tokens : 2 * tokens, part], lse, delta


def window_kernel(stage):
    dq, dq_other, parts = stage.kept[0], stage.kept[1], stage.kept[2:]
    row = lax.axis_index("ha")
    column, half, place = place_in_row()
    first, last = place == 0, place == HALF - 1
    lower, upper = half == 0, half == 1
    groups = (
        ((0, 1, 2), (None, row > 0, row < lax.axis_size("ha") - 1), None),
        ((3,), (jnp.logical_not(first & upper),), first & lower),
        ((4,), (jnp.logical_not(last & lower),), last & upper),
    )
    width = dq.shape[1]
    heads = width // HEAD
    qu, other, dq_far, dq_other_far = (stage.get(n) for n in range(4))
    tiles = [stage.get(n) for n in range(4, 9)]
    for head in range(heads):
        part = cols(head)
        grad, grad_other = dq_far[:, part], dq_other_far[:, part]
        mine, theirs = read_query(qu, part), read_query(other, part)
        for members, there, swapped in groups:
            query, upstream, lse, delta = (
                mine
                if swapped is None
                else tuple(lax.select(swapped, b, a) for a, b in zip(mine, theirs))
            )
            tokens = tiles[members[0]].shape[1]
            bound = jnp.concatenate(
                [
                    jnp.broadcast_to(
                        lse if valid is None else jnp.where(valid, lse, jnp.inf), (tokens, HEAD)
                    )
                    for valid in there
                ],
                axis=0,
            )
            dkey, dval, dquery = block_grads(
                jnp.concatenate([tiles[n][0, :, part] for n in members], axis=0),
                jnp.concatenate([tiles[n][1, :, part] for n in members], axis=0),
                query,
                upstream,
                bound,
                delta,
            )
            for step, n in enumerate(members):
                low = step * tokens
                parts[n][0, :, part] = dkey[low : low + tokens]
                parts[n][1, :, part] = dval[low : low + tokens]
            if swapped is None:
                grad = grad + dquery
            else:
                grad = grad + jnp.where(swapped, 0.0, dquery)
                grad_other = grad_other + jnp.where(swapped, dquery, 0.0)
        dq[:, part] = grad
        dq_other[:, part] = grad_other
        if head in (heads // 2, heads - 1):
            for n in range(7):
                stage.put_heads(n, 0 if head < heads - 1 else heads // 2 + 1, head + 1)


def far_kernel(stage):
    back, own_dq, other_dq = stage.kept
    heads = own_dq.shape[1] // HEAD
    table = stage.get(0)
    sources = stage.get(1), stage.get(2)
    got = stage.get(3)
    for head in range(heads):
        part = cols(head)
        for side, grad in enumerate((own_dq, other_dq)):
            query, upstream, lse, delta = read_query(sources[side], part)
            low, mid, high = 2 * side * KEYS, (2 * side + 1) * KEYS, (2 * side + 2) * KEYS
            bound = jnp.concatenate(
                [
                    jnp.broadcast_to(
                        jnp.where(table[4 + side, peer] > 0, lse, jnp.inf), (KEYS, HEAD)
                    )
                    for peer in range(HALF)
                ],
                axis=0,
            )
            dkey, dval, dquery = block_grads(
                got[:, low:mid, part].reshape(HALF * KEYS, HEAD),
                got[:, mid:high, part].reshape(HALF * KEYS, HEAD),
                query,
                upstream,
                bound,
                delta,
            )
            back[:, low:mid, part] = dkey.reshape(HALF, KEYS, HEAD)
            back[:, mid:high, part] = dval.reshape(HALF, KEYS, HEAD)
            grad[:, part] = dquery
        if head in (heads // 2, heads - 1):
            for n in range(3):
                stage.put_heads(n, 0 if head < heads - 1 else heads // 2 + 1, head + 1)


def query_sum_kernel(stage):
    gains, raw, first, second = (stage.get(n) for n in range(4))
    dq, dots = stage.kept
    total = jnp.zeros((HEAD, HEAD), F32)
    for head in range(dq.shape[1] // HEAD):
        part = cols(head)
        grad = (first[:, part] + second[:, part]).astype(BF16)
        dq[:, part] = grad
        total = total + gains[0:1, part] * grad.astype(F32) * raw[:, part].astype(F32)
    dots[...] = row_sums(total)
    stage.put(0)
    stage.put(1)


def sum_kernel(stage):
    total = stage.extra[0]
    dk, dv, dots = stage.kept
    table, gains, raw, own, below, above, right, left, back, q_dots = (
        stage.get(n) for n in range(10)
    )
    dots[0:1, :] = q_dots[...]
    for kind in range(2):
        total[kind, 0:KEYS] = sum(ref[kind, 0:KEYS].astype(F32) for ref in (own, below, above))
        total[kind, KEYS:] = sum(
            ref[kind, KEYS:].astype(F32) for ref in (own, below, above)
        ) + (right[kind].astype(F32) + left[kind].astype(F32))
    for peer in range(HALF):
        for side in range(2):

            @pl.when(table[2 + side, peer] > 0)
            def _():
                start = pl.multiple_of(table[side, peer] * KEYS, KEYS)
                for kind in range(2):
                    low = (2 * side + kind) * KEYS
                    total[kind, pl.ds(start, KEYS), :] += back[peer, low : low + KEYS, :].astype(F32)

    dot = jnp.zeros((HEAD, HEAD), F32)
    for head in range(dk.shape[1] // HEAD):
        part = cols(head)
        grad = total[0, :, part].astype(BF16)
        dk[:, part] = grad
        dv[:, part] = total[1, :, part].astype(BF16)
        dot = dot + gains[1:2, part] * grad.astype(F32) * raw[:, part].astype(F32)
    dots[1:2, :] = row_sums(dot)
    for n in (2, 0, 1):
        stage.put(n)


def last_kernel(full_width, stage):
    gains, squares, dots = (stage.get(n) for n in range(3))
    for place in range(2):
        grad, raw, out = stage.get(3 + place), stage.get(5 + place), stage.kept[place]
        row = norm_rate(squares[place : place + 1, :], full_width)
        rate = tall(row)
        pull = tall(row * row * row * dots[place : place + 1, :] / full_width)
        for head in range(out.shape[1] // HEAD):
            part = cols(head)
            out[:, part] = (
                rate * gains[place : place + 1, part] * grad[:, part].astype(F32)
                - raw[:, part].astype(F32) * pull
            ).astype(BF16)
        stage.put(place)


def body(q_raw, k_raw, values, upstream, outputs, logsumexp, gain_q, gain_k, far_list):
    columns = lax.axis_size("wa")
    q_tile, k_tile, v_tile = q_raw[0, 0], k_raw[0, 0], values[0, 0]
    up_tile, out_tile = upstream[0, 0], outputs[0, 0]
    tokens, width = q_tile.shape
    full_width = width * lax.axis_size("hd")
    lse_row = logsumexp[0, 0].reshape(1, width)

    tile_pair = shape((2, tokens, width), BF16)
    slots = shape((HALF, 4 * KEYS, width), BF16)
    wide = shape((tokens, width), F32)
    narrow = shape((tokens, width), BF16)
    flops = 10 * tokens * tokens * width

    groups = [[h * HALF + z for z in range(HALF)] for h in range(2)]
    swap = [(c, (c + HALF) % columns) for c in range(columns)]

    def exchange(array):
        return lax.all_to_all(array, "wa", 0, 0, axis_index_groups=groups, tiled=True)

    def shifted(array, step):
        count = lax.axis_size("ha")
        first, last = max(0, -step), min(count, count - step)
        return lax.ppermute(array, "ha", [(i, i + step) for i in range(first, last)])

    def ringed(array, step):
        ring = [(c, c // HALF * HALF + (c + step) % HALF) for c in range(columns)]
        return lax.ppermute(array, "wa", ring)

    rest_pair = shape((2, tokens - KEYS, width), BF16)
    row = shape((1, tokens), F32)
    pair_row = shape((2, tokens), F32)
    squares, gains, table = staged_call(
        front_kernel, (pair_row, shape((2, width), F32)),
        (q_tile, k_tile, gain_q, gain_k, jnp.transpose(far_list, (2, 0, 1))), 2,
        made=(shape((6, HALF), jnp.int32),),
    )
    squares = lax.psum(squares, "hd")
    kv, rest, packed = staged_call(
        functools.partial(pack_kernel, full_width), (tile_pair, rest_pair, slots),
        (squares, gains, k_tile, v_tile, table), 4,
    )
    got = exchange(packed)
    (qu,) = staged_call(
        functools.partial(query_kernel, full_width), (shape((2 * tokens + 16, width), BF16),),
        (squares, gains, lse_row, q_tile, up_tile, out_tile), 1,
    )
    other = lax.ppermute(qu, "wa", swap)
    above = shifted(kv, 1)
    below = shifted(kv, -1)
    left = ringed(rest, 1)
    right = ringed(rest, -1)

    got, other, above, below, left, right = lax.optimization_barrier(
        (got, other, above, below, left, right)
    )
    back_slots, dq_far, dq_other = staged_call(
        far_kernel, (slots, wide, wide), (table, qu, other, got), 6, flops=4 * flops, limit=ROOMY
    )
    back = exchange(back_slots)
    dq_own, dq_other, own_part, up_part, down_part, left_part, right_part = staged_call(
        window_kernel, (wide, wide) + (tile_pair,) * 3 + (rest_pair,) * 2,
        (qu, other, dq_far, dq_other, kv, above, below, left, right), 14, flops=5 * flops, limit=ROOMY,
    )
    dq_got = lax.ppermute(dq_other, "wa", swap)
    from_below = shifted(up_part, -1)
    from_above = shifted(down_part, 1)
    from_right = ringed(left_part, -1)
    from_left = ringed(right_part, 1)

    dq_norm, q_dots = staged_call(query_sum_kernel, (narrow, row), (gains, q_tile, dq_own, dq_got), 2)
    dk_norm, dv_tile, dots = staged_call(
        sum_kernel,
        (narrow, narrow, pair_row),
        (
            table, gains, k_tile, own_part, from_below, from_above, from_right, from_left, back,
            q_dots,
        ),
        3,
        extra=(shape((2, tokens, width), F32),),
        limit=ROOMY,
    )
    dq_tile, dk_tile = staged_call(
        functools.partial(last_kernel, full_width), (narrow, narrow),
        (gains, squares, lax.psum(dots, "hd"), dq_norm, dk_norm, q_tile, k_tile), 2,
    )
    return (dq_tile[None, None], dk_tile[None, None], dv_tile[None, None])


def solution(mesh):
    tile = P("ha", "wa", None, "hd")
    return jax.shard_map(
        body,
        mesh=mesh,
        in_specs=(
            tile, tile, tile, tile, tile,
            P("ha", "wa", "hd", None), P("hd"), P("hd"), P("ha", None, None),
        ),
        out_specs=(tile, tile, tile),
        check_vma=False,
    )
```
